32 devices in a mesh: sub: 4 (over z), row: 8 (over y, x, core).
Axes of the slice: x: 2, y: 2, z: 4, core: 2. Of those that a mesh axis runs over, the one named last changes fastest.
Arguments:
- spectra: bfloat16 [4, 65536, 256], P('sub', 'row')
- mass_blocks: bfloat16 [4, 512, 9, 128, 128], P('sub', 'row'), may hold values from -0.1875 to 0.1875
- offsets: int32 [4, 512, 9], P('sub', 'row'), may hold values from -16 to 16
- counts: int32 [4], P('sub'), may hold values from 1 to 65536, 183500 in all
Outputs:
- weighted_modes: bfloat16 [4, 65536, 192], P('sub', 'row')
The draws below stay inside these ranges and needn't reach their ends.
Inputs may be any that keep to these rules, and one draw needn't show every extreme that they name: `counts`: rows at or past a subdomain's count hold no data; the largest count is exactly 65536.
All inputs are finite; a program needn't handle non-finite values. No bound on the sum of `counts` on one device may be relied on, other than what follows from the above.
Results may differ from the reference program's by a relative error of at most 0.001.
The reference program's roundings to bfloat16 on the way (of `masked`, `weighted` and `projector`) count: a program that leaves them out, or rounds other values in their place, can miss the bound.
Values may be sent and summed in bfloat16 or wider, within the bound.
A program may use at most 256 MiB of HBM per device.

```python
import math
import jax
import jax.numpy as jnp
import numpy as np
from jax import lax

BLK = 64
RANK = 48
FREQ = 2
BS = 128
NBR = 9
ITERS = 5
HB = 16
ROWS = 65536
BLOCKS = 512
SUBS = 4
COLS = 256


def draw_spectra(key, part):
    key_base, key_rows, key_cols = jax.random.split(key, 3)
    row_scale = jnp.exp(jax.random.uniform(key_rows, (SUBS, ROWS, 1), jnp.float32, math.log(0.3), math.log(3.0)))
    col_scale = jnp.exp(jax.random.uniform(key_cols, (1, 1, COLS), jnp.float32, math.log(0.4), math.log(4.0)))
    base = jax.random.normal(key_base, (SUBS, ROWS, COLS), jnp.float32)
    values = jnp.clip(base * row_scale * col_scale, -40.0, 40.0)
    return values.astype(jnp.bfloat16)


def touch_ends(drawn, own_key, least, largest):
    spot = [jax.random.randint(jax.random.fold_in(own_key, axis), (), 0, length) for axis, length in enumerate(drawn.shape)]
    main_axis = drawn.shape.index(max(drawn.shape))
    neighbour = spot[:main_axis] + [(spot[main_axis] + 1) % drawn.shape[main_axis]] + spot[main_axis + 1:]
    return drawn.at[tuple(spot)].set(least).at[tuple(neighbour)].set(largest)


def shard_levels(stream_key, dims, pieces, least, top_value):
    def one(axis_at, blocks):
        draws = jax.random.uniform(jax.random.fold_in(jax.random.fold_in(stream_key, 6), axis_at), (blocks,), jnp.float32, least / len(pieces), top_value / len(pieces))
        return jnp.repeat(jnp.exp(draws), dims[axis_at] // blocks).reshape((-1,) + (1,) * (len(dims) - axis_at - 1))

    level = one(*pieces[0])
    for cut in pieces[1:]:
        level = level * one(*cut)
    return level


def profile(amount, total, limit, lean):
    portions = [(1 << 20) // math.isqrt(grade ** lean) + 1 for grade in range(2, amount + 1)]
    surplus, given = total - limit - (amount - 1), [1] * (amount - 1)
    while surplus > 0:
        movable = [i for i in range(amount - 1) if given[i] < limit]
        pool, left = sum([portions[i] for i in movable]), surplus
        for i in movable:
            extra = min(limit - given[i], max(1, left * portions[i] // pool), surplus)
            given[i] = given[i] + extra
            surplus = surplus - extra
    return np.array([limit] + given)


def ragged_sizes(rng, count, total, bound, skew):
    if count == 2:
        one = jax.random.randint(rng, (), max(1, total - bound), min(bound, total - 1) + 1)
        return jnp.stack([one, total - one])
    sizes = jnp.asarray(profile(count, total, bound, skew), jnp.int32)
    couples = (count - 1) // 2
    giver, receiver = sizes[1:1 + 2 * couples:2], sizes[2:2 + 2 * couples:2]
    margin = jnp.minimum(giver - 1, bound - receiver)
    shifted = jax.random.randint(jax.random.fold_in(rng, 1), (couples,), 0, 1 << 20) % (margin + 1)
    sizes = sizes.at[1:1 + 2 * couples:2].set(giver - shifted).at[2:2 + 2 * couples:2].set(receiver + shifted)
    return sizes[jax.random.permutation(jax.random.fold_in(rng, 2), count)]


def centred(key, extent, spread, reach, pieces=(), kind=jnp.bfloat16):
    gain = shard_levels(key, extent, pieces, -0.22, 0.18) if pieces else 1.0
    drawn = jax.random.normal(key, extent, jnp.float32) * spread * gain
    return jnp.minimum(jnp.maximum(drawn, -reach), reach).astype(kind)


def setup_inputs(seed: int = 0) -> dict:
    streams_of = jax.random.split(jax.random.key(seed), 5)
    spectra = draw_spectra(jax.random.fold_in(streams_of[4], 71), 0)
    mass_blocks = centred(streams_of[1], (SUBS, BLOCKS, NBR, BS, BS), (NBR * BS) ** -0.5, 0.1875, ((0, 4), (1, 8)))
    offsets = touch_ends(jax.random.randint(streams_of[2], (SUBS, BLOCKS, NBR), 0 - HB, HB + 1), jax.random.fold_in(streams_of[2], 1), 0 - HB, HB).astype(jnp.int32)
    counts = ragged_sizes(streams_of[3], SUBS, SUBS * ROWS * 7 // 10, ROWS, 0).astype(jnp.int32)
    return {"spectra": spectra, "mass_blocks": mass_blocks, "offsets": offsets, "counts": counts}


def weigh_subdomain(spectra_sub, mass_sub, offsets_sub, live_count):
    row_count = spectra_sub.shape[0]
    live_rows = (jnp.arange(row_count, dtype=jnp.int32) < live_count)[:, None]
    masked = jnp.where(live_rows, spectra_sub, jnp.zeros((), spectra_sub.dtype))
    halo_rows = HB * BS
    padded = jnp.pad(masked, ((halo_rows, halo_rows), (0, 0)))
    block_count = row_count // BS
    blocks = padded.reshape(block_count + 2 * HB, BS, COLS)
    block_index = (jnp.arange(block_count, dtype=jnp.int32)[:, None] + offsets_sub + HB).astype(jnp.int32)
    summed = jnp.zeros((block_count, BS, COLS), jnp.float32)
    for slot in range(NBR):
        picked = jnp.take(blocks, block_index[:, slot], axis=0).astype(jnp.float32)
        summed = summed + jnp.einsum('bij,bjc->bic', mass_sub[:, slot].astype(jnp.float32), picked)
    weighted = jnp.where(live_rows, summed.reshape(row_count, COLS), 0.0).astype(jnp.bfloat16)
    columns = weighted.reshape(row_count, FREQ, 2 * BLK).astype(jnp.float32)
    gram = jnp.einsum('rfc,rfd->fcd', columns, columns)
    return (weighted, gram)

def whiten(gram):
    half_width = BLK
    g_real = gram[:, :half_width, :half_width] + gram[:, half_width:, half_width:]
    g_imag = gram[:, :half_width, half_width:] - gram[:, half_width:, :half_width]
    realified = jnp.concatenate([jnp.concatenate([g_real, -g_imag], 2), jnp.concatenate([g_imag, g_real], 2)], 1)
    scaled = realified / jnp.sqrt(lax.optimization_barrier(jnp.sum(realified * realified, axis=(1, 2), keepdims=True)) + 1e-06)
    identity = jnp.broadcast_to(jnp.eye(2 * half_width, dtype=jnp.float32), scaled.shape)
    iterate = scaled
    whitener = identity
    for step in range(ITERS):
        correction = 1.5 * identity - 0.5 * jnp.einsum('fij,fjk->fik', whitener, iterate, precision=lax.Precision.HIGHEST)
        iterate = jnp.einsum('fij,fjk->fik', iterate, correction, precision=lax.Precision.HIGHEST)
        whitener = jnp.einsum('fij,fjk->fik', correction, whitener, precision=lax.Precision.HIGHEST)
    r_real = whitener[:, :half_width, :RANK]
    r_imag = whitener[:, half_width:, :RANK]
    projector = jnp.concatenate([jnp.concatenate([r_real, r_imag], 2), jnp.concatenate([-r_imag, r_real], 2)], 1)
    return projector.astype(jnp.bfloat16)

def reference(spectra, mass_blocks, offsets, counts):

    def one_subdomain(items):
        return weigh_subdomain(items[0], items[1], items[2], items[3])
    weighted, grams = lax.map(one_subdomain, (spectra, mass_blocks, offsets, counts))
    gram = lax.optimization_barrier(jnp.sum(grams, axis=0))
    projector = whiten(gram).astype(jnp.float32)

    def project(weighted_sub):
        columns = weighted_sub.reshape(ROWS, FREQ, 2 * BLK).astype(jnp.float32)
        modes = jnp.einsum('rfc,fcd->rfd', columns, projector)
        return modes.reshape(ROWS, FREQ * 2 * RANK).astype(jnp.bfloat16)
    return lax.map(project, weighted)
```

```python
import functools

import jax
import jax.numpy as jnp
from jax import lax
from jax.experimental import pallas as pl
from jax.experimental.pallas import tpu as pltpu
from jax.sharding import PartitionSpec as P

RANK = 48
FREQ = 2
ITERS = 5
HB = 16
GROUP = 4
MESH = pl.DeviceIdType.MESH


def peer_copy(src, dst, send, recv, axis, index):
    return pltpu.make_async_remote_copy(
        src_ref=src, dst_ref=dst, send_sem=send, recv_sem=recv,
        device_id={axis: index}, device_id_type=MESH,
    )


def live_mask(first, shape, count):
    rows = first + lax.broadcasted_iota(jnp.int32, shape, 0)
    return rows < count


def realify(part):
    width = part.shape[0]
    half = width // 2
    swapped = pltpu.roll(pltpu.roll(part, half, 0), half, 1)
    low_row = lax.broadcasted_iota(jnp.int32, part.shape, 0) < half
    low_col = lax.broadcasted_iota(jnp.int32, part.shape, 1) < half
    return swapped + jnp.where(low_row == low_col, part, -part)


def weigh_kernel(
    n_row, n_sub, count_ref, offsets_ref, spectra_ref, mass_ref,
    weighted_ref, total_ref,
    own, low, high, gram, packed, landed, subs, gathered,
    load_sem, halo_send, halo_recv,
    first_send, first_recv, second_send, second_recv, third_send, third_recv,
):
    step = pl.program_id(0)
    steps = pl.num_programs(0)
    row = lax.axis_index("row")
    sub = lax.axis_index("sub")
    blocks, size, cols = own.shape
    reach = HB
    slots = mass_ref.shape[1]
    edge = reach // GROUP
    group = lax.rem(step + edge, steps)
    count = count_ref[0]
    base = row * blocks

    to_next = peer_copy(
        spectra_ref.at[pl.ds(blocks - reach, reach)], low.at[pl.ds(0, reach)],
        halo_send.at[0], halo_recv.at[0], "row", lax.rem(row + 1, n_row))
    to_prev = peer_copy(
        spectra_ref.at[pl.ds(0, reach)], high.at[pl.ds(2 * reach, reach)],
        halo_send.at[1], halo_recv.at[1], "row", lax.rem(row + n_row - 1, n_row))

    @pl.when(step == 0)
    def _():
        barrier = pltpu.get_barrier_semaphore()
        for j in range(1, n_row):
            pl.semaphore_signal(barrier, inc=1, device_id={"row": lax.rem(row + j, n_row)},
                                device_id_type=MESH)
        for j in range(1, n_sub):
            pl.semaphore_signal(barrier, inc=1, device_id={"sub": lax.rem(sub + j, n_sub)},
                                device_id_type=MESH)
        load = pltpu.make_async_copy(spectra_ref, own, load_sem)
        load.start()
        gram[...] = jnp.zeros_like(gram)

        @pl.when(row == 0)
        def _():
            low[pl.ds(0, reach)] = jnp.zeros((reach, size, cols), low.dtype)

        @pl.when(row == n_row - 1)
        def _():
            high[pl.ds(2 * reach, reach)] = jnp.zeros((reach, size, cols), high.dtype)

        pl.semaphore_wait(barrier, n_row + n_sub - 2)

        @pl.when(row < n_row - 1)
        def _():
            to_next.start()

        @pl.when(row > 0)
        def _():
            to_prev.start()

        load.wait()

        def clear(b, carry):
            for side in range(2):
                at = b + side * (blocks - 2 * reach)
                live = live_mask((base + at) * size, (size, cols), count)
                value = jnp.where(live, own[at], jnp.zeros((), own.dtype))
                own[at] = value
                if side == 0:
                    low[b + reach] = value
                else:
                    high[b] = value
            return carry

        lax.fori_loop(0, 2 * reach, clear, 0)

    def clear_halo(buffer, start, first_block):
        def body(b, carry):
            live = live_mask((first_block + b) * size, (size, cols), count)
            buffer[start + b] = jnp.where(live, buffer[start + b], jnp.zeros((), buffer.dtype))
            return carry
        lax.fori_loop(0, reach, body, 0)

    @pl.when(step == steps - 2 * edge)
    def _():
        @pl.when(row < n_row - 1)
        def _():
            to_prev.wait_recv()
        clear_halo(high, 2 * reach, base + blocks)

    @pl.when(step == steps - edge)
    def _():
        @pl.when(row > 0)
        def _():
            to_next.wait_recv()
        clear_halo(low, 0, base - reach)

    def weigh(buffer, shift):
        for r in range(GROUP):
            at = group * GROUP + r
            picks = [buffer[at + shift + offsets_ref[k, at]] for k in range(slots)]
            factor = jnp.concatenate([mass_ref[r, k] for k in range(slots)], axis=1)
            summed = jnp.dot(factor, jnp.concatenate(picks, axis=0),
                             preferred_element_type=jnp.float32)
            live = live_mask((base + at) * size, (size, cols), count)
            weighted_ref[r] = jnp.where(live, summed, 0.0).astype(weighted_ref.dtype)

    @pl.when(step < steps - 2 * edge)
    def _():
        weigh(own, 0)

    @pl.when(jnp.logical_and(step >= steps - 2 * edge, step < steps - edge))
    def _():
        weigh(high, 2 * reach - blocks)

    @pl.when(step >= steps - edge)
    def _():
        weigh(low, reach)

    z = weighted_ref[...].reshape(GROUP * size, cols)
    gram[...] += lax.dot_general(z, z, (((0,), (0,)), ((), ())),
                                 preferred_element_type=jnp.float32)

    @pl.when(step == steps - 1)
    def _():
        width = cols // FREQ
        depth = packed.shape[1]
        for f in range(FREQ):
            cut = slice(f * width, (f + 1) * width)
            top = realify(gram[cut, cut])[: width // 2]
            pieces = (width // 2) // depth
            packed[f * pieces : (f + 1) * pieces] = top.reshape(pieces, depth, width)

        def spread(n, axis, me, src, slot_of, send, recv):
            copies = []
            for j in range(1, n):
                peer = lax.rem(me + j, n)
                copy = peer_copy(src(peer), slot_of(me), send.at[j], recv.at[j], axis, peer)
                copy.start()
                copies.append(copy)
            for j in range(1, n):
                peer = lax.rem(me + n - j, n)
                peer_copy(src(peer), slot_of(peer), send.at[j], recv.at[j], axis, peer).wait_recv()
            return copies

        first = spread(n_row, "row", row, lambda p: packed.at[p], lambda s: landed.at[s],
                       first_send, first_recv)
        landed[row] = packed[row]
        partial = landed[0]
        for j in range(1, n_row):
            partial = partial + landed[j]
        subs[sub] = partial
        second = spread(n_sub, "sub", sub, lambda p: subs.at[sub], lambda s: subs.at[s],
                        second_send, second_recv)
        whole = subs[0]
        for j in range(1, n_sub):
            whole = whole + subs[j]
        gathered[row] = whole
        third = spread(n_row, "row", row, lambda p: gathered.at[row], lambda s: gathered.at[s],
                       third_send, third_recv)
        total_ref[...] = gathered[...]

        @pl.when(row < n_row - 1)
        def _():
            to_next.wait_send()

        @pl.when(row > 0)
        def _():
            to_prev.wait_send()

        for copy in first + second + third:
            copy.wait_send()


def weigh_call(n_row, n_sub, counts, offsets, spectra, mass_blocks):
    blocks, size, cols = spectra.shape
    slots = mass_blocks.shape[1]
    steps = blocks // GROUP
    edge = HB // GROUP
    width = cols // FREQ
    depth = FREQ * (width // 2) // n_row
    dma = pltpu.SemaphoreType.DMA

    def place(i):
        return lax.rem(i + edge, steps)

    return pl.pallas_call(
        functools.partial(weigh_kernel, n_row, n_sub),
        grid=(steps,),
        out_shape=(
            jax.ShapeDtypeStruct((blocks, size, cols), jnp.bfloat16),
            jax.ShapeDtypeStruct((n_row, depth, width), jnp.float32),
        ),
        in_specs=[
            pl.BlockSpec(memory_space=pltpu.SMEM),
            pl.BlockSpec(memory_space=pltpu.SMEM),
            pl.BlockSpec(memory_space=pl.ANY),
            pl.BlockSpec((GROUP, slots, size, size), lambda i: (place(i), 0, 0, 0)),
        ],
        out_specs=(
            pl.BlockSpec((GROUP, size, cols), lambda i: (place(i), 0, 0)),
            pl.BlockSpec(memory_space=pltpu.VMEM),
        ),
        scratch_shapes=[
            pltpu.VMEM((blocks, size, cols), jnp.bfloat16),
            pltpu.VMEM((3 * HB, size, cols), jnp.bfloat16),
            pltpu.VMEM((3 * HB, size, cols), jnp.bfloat16),
            pltpu.VMEM((cols, cols), jnp.float32),
            pltpu.VMEM((n_row, depth, width), jnp.float32),
            pltpu.VMEM((n_row, depth, width), jnp.float32),
            pltpu.VMEM((n_sub, depth, width), jnp.float32),
            pltpu.VMEM((n_row, depth, width), jnp.float32),
            dma, dma((2,)), dma((2,)),
            dma((n_row,)), dma((n_row,)),
            dma((n_sub,)), dma((n_sub,)),
            dma((n_row,)), dma((n_row,)),
        ],
        compiler_params=pltpu.CompilerParams(
            collective_id=0, has_side_effects=True, vmem_limit_bytes=40 << 20,
            dimension_semantics=("arbitrary",),
        ),
        name="weigh",
    )(counts, offsets, spectra, mass_blocks)


def spot(shape, shift, least, most):
    source = lax.broadcasted_iota(jnp.int32, shape, 0)
    target = lax.broadcasted_iota(jnp.int32, shape, 1)
    hit = (target == source + shift) & (source >= least) & (source < most)
    return jnp.where(hit, 1.0, 0.0).astype(jnp.bfloat16)


def project_kernel(top_ref, z_ref, modes_ref, projector):
    @pl.when(pl.program_id(0) == 0)
    def _():
        width = top_ref.shape[1]
        half = width // 2
        out_cols = projector.shape[0]
        exact = functools.partial(
            jnp.dot, precision=lax.Precision.HIGHEST, preferred_element_type=jnp.float32)
        rows = lax.broadcasted_iota(jnp.int32, (width, width), 0)
        columns = lax.broadcasted_iota(jnp.int32, (width, width), 1)
        lift = jnp.where(rows == columns, 1.5, 0.0)
        iterates = []
        for f in range(FREQ):
            top = top_ref[f * half : (f + 1) * half]
            bottom = pltpu.roll(top, half, 1)
            bottom = jnp.where(columns[:half] < half, -bottom, bottom)
            full = jnp.concatenate([top, bottom], axis=0)
            norm = jnp.sqrt(jnp.sum(full * full, axis=(0, 1), keepdims=True) + 1e-06)
            iterates.append(full / norm)
        whiteners = [None] * FREQ
        for at in range(ITERS):
            for f in range(FREQ):
                both = iterates[f] if at == 0 else exact(whiteners[f], iterates[f])
                fix = lift - 0.5 * both
                if at < ITERS - 1:
                    iterates[f] = exact(iterates[f], fix)
                whiteners[f] = fix if at == 0 else exact(fix, whiteners[f])
        for f in range(FREQ):
            straight = jnp.where(rows < half, whiteners[f], -whiteners[f])
            crossed = pltpu.roll(whiteners[f], half, 0)
            shape = (width, out_cols)
            value = jnp.dot(
                straight.astype(jnp.bfloat16), spot(shape, 2 * f * RANK, 0, RANK),
                preferred_element_type=jnp.float32)
            value += jnp.dot(
                crossed.astype(jnp.bfloat16), spot(shape, (2 * f + 1) * RANK, 0, RANK),
                preferred_element_type=jnp.float32)
            projector[:, f * width : (f + 1) * width] = value.T.astype(jnp.bfloat16)

    modes_ref[...] = lax.dot_general(
        projector[...], z_ref[...], (((1,), (1,)), ((), ())),
        preferred_element_type=jnp.float32).astype(modes_ref.dtype)


def project_call(top, weighted):
    rows, cols = weighted.shape
    out_cols = FREQ * 2 * RANK
    tile = 1024
    return pl.pallas_call(
        project_kernel,
        grid=(rows // tile,),
        out_shape=jax.ShapeDtypeStruct((out_cols, rows), jnp.bfloat16),
        in_specs=[
            pl.BlockSpec(top.shape, lambda i: (0, 0)),
            pl.BlockSpec((tile, cols), lambda i: (i, 0)),
        ],
        out_specs=pl.BlockSpec((out_cols, tile), lambda i: (0, i)),
        scratch_shapes=[pltpu.VMEM((out_cols, cols), jnp.bfloat16)],
        compiler_params=pltpu.CompilerParams(
            vmem_limit_bytes=32 << 20, dimension_semantics=("arbitrary",)),
        name="project",
    )(top, weighted)


def local(n_row, n_sub, spectra, mass_blocks, offsets, counts):
    rows, cols = spectra.shape[1:]
    size = mass_blocks.shape[3]
    weighted, total = weigh_call(
        n_row, n_sub, counts, offsets[0].T,
        spectra[0].reshape(rows // size, size, cols), mass_blocks[0])
    width = cols // FREQ
    modes = project_call(
        total.reshape(FREQ * width // 2, width), weighted.reshape(rows, cols))
    return modes.T[None]


def solution(mesh):
    return jax.shard_map(
        functools.partial(local, mesh.shape["row"], mesh.shape["sub"]),
        mesh=mesh,
        in_specs=(
            P("sub", "row", None),
            P("sub", "row", None, None, None),
            P("sub", "row", None),
            P("sub"),
        ),
        out_specs=P("sub", "row", None),
        check_vma=False,
    )
```

```python
import functools

import jax
import jax.numpy as jnp
from jax import lax
from jax.experimental import pallas as pl
from jax.experimental.pallas import tpu as pltpu
from jax.sharding import PartitionSpec as P

RANK = 48
FREQ = 2
ITERS = 5
HB = 16
GROUP = 4
MESH = pl.DeviceIdType.MESH


def peer_copy(src, dst, send, recv, axis, index):
    return pltpu.make_async_remote_copy(
        src_ref=src, dst_ref=dst, send_sem=send, recv_sem=recv,
        device_id={axis: index}, device_id_type=MESH,
    )


def masked(value, rows, first, count):
    live = jnp.clip(count - first, 0, value.shape[0]).astype(jnp.float32)
    bound = jnp.full(value.shape, live, jnp.float32).astype(jnp.bfloat16)
    return jnp.where(rows < bound, value, jnp.zeros((), value.dtype))


def realify(part):
    width = part.shape[0]
    half = width // 2
    swapped = pltpu.roll(pltpu.roll(part, half, 0), half, 1)
    low_row = lax.broadcasted_iota(jnp.int32, part.shape, 0) < half
    low_col = lax.broadcasted_iota(jnp.int32, part.shape, 1) < half
    return swapped + jnp.where(low_row == low_col, part, -part)


def place(step, steps):
    edge, pair = HB // GROUP, HB // GROUP // 2
    inside = steps - 2 * edge
    late = step - inside
    turn = late // pair
    within = late % pair
    outer = jnp.where(
        turn == 0, steps - edge + within,
        jnp.where(turn == 1, pair + within, jnp.where(turn == 2, steps - pair + within, within)))
    return jnp.where(step < inside, step + edge, outer)


def weigh_kernel(
    n_row, n_sub, count_ref, offsets_ref, spectra_ref, mass_ref,
    weighted_ref, total_ref,
    own, low_near, low_far, high_near, high_far, rows_in, gram, packed, landed, subs, gathered,
    load_sem, fill_sem, halo_send, halo_recv,
    first_send, first_recv, second_send, second_recv, third_send, third_recv,
):
    step = pl.program_id(0)
    steps = pl.num_programs(0)
    row = lax.axis_index("row")
    sub = lax.axis_index("sub")
    blocks, size, cols = own.shape
    reach = HB
    slots = mass_ref.shape[1]
    near = reach // 2
    pair = near // GROUP
    group = place(step, steps)
    count = count_ref[0]
    base = row * blocks
    after = lax.rem(row + 1, n_row)
    before = lax.rem(row + n_row - 1, n_row)

    def halo(src_at, dst, dst_at, sem, peer):
        return peer_copy(
            spectra_ref.at[pl.ds(src_at, near)], dst.at[pl.ds(dst_at, near)],
            halo_send.at[sem], halo_recv.at[sem], "row", peer)

    to_next = [halo(blocks - near, low_near, 0, 0, after),
               halo(blocks - reach, low_far, 0, 1, after)]
    to_prev = [halo(0, high_near, 2 * reach, 2, before),
               halo(near, high_far, 2 * reach, 3, before)]
    most = 2 * reach
    part = reach + near
    fills = [
        pltpu.make_async_copy(own.at[pl.ds(at, length)], buffer.at[pl.ds(to, length)],
                              fill_sem.at[sem])
        for sem, (at, length, buffer, to) in enumerate((
            (blocks - most, most, high_near, 0),
            (0, most, low_near, near),
            (blocks - part, part, high_far, 0),
            (0, part, low_far, reach),
        ))
    ]

    @pl.when(step == 0)
    def _():
        barrier = pltpu.get_barrier_semaphore()
        for j in range(1, n_row):
            pl.semaphore_signal(barrier, inc=1, device_id={"row": lax.rem(row + j, n_row)},
                                device_id_type=MESH)
        for j in range(1, n_sub):
            pl.semaphore_signal(barrier, inc=1, device_id={"sub": lax.rem(sub + j, n_sub)},
                                device_id_type=MESH)
        load = pltpu.make_async_copy(spectra_ref, own, load_sem)
        load.start()
        gram[...] = jnp.zeros_like(gram)
        rows_in[...] = lax.broadcasted_iota(jnp.int32, (size, cols), 0).astype(
            jnp.float32).astype(jnp.bfloat16)

        @pl.when(row == 0)
        def _():
            low_near[pl.ds(0, near)] = jnp.zeros((near, size, cols), low_near.dtype)
            low_far[pl.ds(0, near)] = jnp.zeros((near, size, cols), low_far.dtype)

        @pl.when(row == n_row - 1)
        def _():
            high_near[pl.ds(most, near)] = jnp.zeros((near, size, cols), high_near.dtype)
            high_far[pl.ds(most, near)] = jnp.zeros((near, size, cols), high_far.dtype)

        pl.semaphore_wait(barrier, n_row + n_sub - 2)

        for at in range(2):
            @pl.when(row < n_row - 1)
            def _():
                to_next[at].start()

            @pl.when(row > 0)
            def _():
                to_prev[at].start()

        load.wait()

        def clear(b, carry):
            own[b] = masked(own[b], rows_in[...], (base + b) * size, count)
            return carry

        lax.fori_loop(0, blocks, clear, 0)
        for fill in fills:
            fill.start()

    def clear_halo(buffer, start, first_block, other=None, other_start=0):
        def body(b, carry):
            value = masked(buffer[start + b], rows_in[...], (first_block + b) * size, count)
            buffer[start + b] = value
            if other is not None:
                other[other_start + b] = value
            return carry
        lax.fori_loop(0, near, body, 0)

    inside = steps - 4 * pair

    @pl.when(step == inside)
    def _():
        @pl.when(row < n_row - 1)
        def _():
            to_prev[0].wait_recv()
        fills[0].wait()
        clear_halo(high_near, most, base + blocks, high_far, part)

    @pl.when(step == inside + pair)
    def _():
        @pl.when(row > 0)
        def _():
            to_next[0].wait_recv()
        fills[1].wait()
        clear_halo(low_near, 0, base - near, low_far, near)

    @pl.when(step == inside + 2 * pair)
    def _():
        @pl.when(row < n_row - 1)
        def _():
            to_prev[1].wait_recv()
        fills[2].wait()
        clear_halo(high_far, most, base + blocks + near)

    @pl.when(step == inside + 3 * pair)
    def _():
        @pl.when(row > 0)
        def _():
            to_next[1].wait_recv()
        fills[3].wait()
        clear_halo(low_far, 0, base - reach)

    def weigh(buffer, shift):
        for r in range(GROUP):
            at = group * GROUP + r
            picks = [buffer[at + shift + offsets_ref[k, at]] for k in range(slots)]
            factor = jnp.concatenate([mass_ref[r, k] for k in range(slots)], axis=1)
            summed = jnp.dot(factor, jnp.concatenate(picks, axis=0),
                             preferred_element_type=jnp.float32)
            weighted_ref[r] = masked(summed.astype(weighted_ref.dtype), rows_in[...],
                                     (base + at) * size, count)

    for least, buffer, shift in (
        (0, own, 0),
        (1, high_near, most - blocks),
        (2, low_near, near),
        (3, high_far, part - blocks),
        (4, low_far, reach),
    ):
        first = 0 if least == 0 else inside + (least - 1) * pair
        last = inside + least * pair

        @pl.when(jnp.logical_and(step >= first, step < last))
        def _():
            weigh(buffer, shift)

    z = weighted_ref[...].reshape(GROUP * size, cols)
    gram[...] += lax.dot_general(z, z, (((0,), (0,)), ((), ())),
                                 preferred_element_type=jnp.float32)

    @pl.when(step == steps - 1)
    def _():
        width = cols // FREQ
        depth = packed.shape[1]
        for f in range(FREQ):
            cut = slice(f * width, (f + 1) * width)
            top = realify(gram[cut, cut])[: width // 2]
            pieces = (width // 2) // depth
            packed[f * pieces : (f + 1) * pieces] = top.reshape(pieces, depth, width)

        def spread(n, axis, me, src, slot_of, send, recv):
            copies = []
            for j in range(1, n):
                peer = lax.rem(me + j, n)
                copy = peer_copy(src(peer), slot_of(me), send.at[j], recv.at[j], axis, peer)
                copy.start()
                copies.append(copy)
            for j in range(1, n):
                peer = lax.rem(me + n - j, n)
                peer_copy(src(peer), slot_of(peer), send.at[j], recv.at[j], axis, peer).wait_recv()
            return copies

        first = spread(n_row, "row", row, lambda p: packed.at[p], lambda s: landed.at[s],
                       first_send, first_recv)
        landed[row] = packed[row]
        partial = landed[0]
        for j in range(1, n_row):
            partial = partial + landed[j]
        subs[sub] = partial
        second = spread(n_sub, "sub", sub, lambda p: subs.at[sub], lambda s: subs.at[s],
                        second_send, second_recv)
        whole = subs[0]
        for j in range(1, n_sub):
            whole = whole + subs[j]
        gathered[row] = whole
        third = spread(n_row, "row", row, lambda p: gathered.at[row], lambda s: gathered.at[s],
                       third_send, third_recv)
        total_ref[...] = gathered[...]

        for at in range(2):
            @pl.when(row < n_row - 1)
            def _():
                to_next[at].wait_send()

            @pl.when(row > 0)
            def _():
                to_prev[at].wait_send()

        for copy in first + second + third:
            copy.wait_send()


def weigh_call(n_row, n_sub, counts, offsets, spectra, mass_blocks):
    blocks, size, cols = spectra.shape
    slots = mass_blocks.shape[1]
    steps = blocks // GROUP
    window = 2 * HB + HB // 2
    width = cols // FREQ
    depth = FREQ * (width // 2) // n_row
    dma = pltpu.SemaphoreType.DMA

    return pl.pallas_call(
        functools.partial(weigh_kernel, n_row, n_sub),
        grid=(steps,),
        out_shape=(
            jax.ShapeDtypeStruct((blocks, size, cols), jnp.bfloat16),
            jax.ShapeDtypeStruct((n_row, depth, width), jnp.float32),
        ),
        in_specs=[
            pl.BlockSpec(memory_space=pltpu.SMEM),
            pl.BlockSpec(memory_space=pltpu.SMEM),
            pl.BlockSpec(memory_space=pltpu.HBM),
            pl.BlockSpec((GROUP, slots, size, size), lambda i: (place(i, steps), 0, 0, 0)),
        ],
        out_specs=(
            pl.BlockSpec((GROUP, size, cols), lambda i: (place(i, steps), 0, 0)),
            pl.BlockSpec(memory_space=pltpu.VMEM),
        ),
        scratch_shapes=[
            pltpu.VMEM((blocks, size, cols), jnp.bfloat16),
            pltpu.VMEM((window, size, cols), jnp.bfloat16),
            pltpu.VMEM((window, size, cols), jnp.bfloat16),
            pltpu.VMEM((window, size, cols), jnp.bfloat16),
            pltpu.VMEM((window, size, cols), jnp.bfloat16),
            pltpu.VMEM((size, cols), jnp.bfloat16),
            pltpu.VMEM((cols, cols), jnp.float32),
            pltpu.VMEM((n_row, depth, width), jnp.float32),
            pltpu.VMEM((n_row, depth, width), jnp.float32),
            pltpu.VMEM((n_sub, depth, width), jnp.float32),
            pltpu.VMEM((n_row, depth, width), jnp.float32),
            dma, dma((4,)), dma((4,)), dma((4,)),
            dma((n_row,)), dma((n_row,)),
            dma((n_sub,)), dma((n_sub,)),
            dma((n_row,)), dma((n_row,)),
        ],
        compiler_params=pltpu.CompilerParams(
            collective_id=0, has_side_effects=True, vmem_limit_bytes=60 << 20,
            dimension_semantics=("arbitrary",),
        ),
        name="weigh",
    )(counts, offsets, spectra, mass_blocks)


def spot(shape, shift, least, most):
    source = lax.broadcasted_iota(jnp.int32, shape, 0)
    target = lax.broadcasted_iota(jnp.int32, shape, 1)
    hit = (target == source + shift) & (source >= least) & (source < most)
    return jnp.where(hit, 1.0, 0.0).astype(jnp.bfloat16)


def halves(value):
    head = value.astype(jnp.bfloat16)
    return head, (value - head.astype(jnp.float32)).astype(jnp.bfloat16)


def exact(first, second):
    a, a_rest = halves(first)
    b, b_rest = halves(second)
    return jnp.dot(
        jnp.concatenate([a, a, a_rest], axis=1), jnp.concatenate([b, b_rest, b], axis=0),
        preferred_element_type=jnp.float32)


def project_kernel(top_ref, z_ref, modes_ref, projector):
    @pl.when(pl.program_id(0) == 0)
    def _():
        width = top_ref.shape[1]
        half = width // 2
        out_cols = projector.shape[0]
        rows = lax.broadcasted_iota(jnp.int32, (width, width), 0)
        columns = lax.broadcasted_iota(jnp.int32, (width, width), 1)
        lift = jnp.where(rows == columns, 1.5, 0.0)
        iterates = []
        for f in range(FREQ):
            top = top_ref[f * half : (f + 1) * half]
            bottom = pltpu.roll(top, half, 1)
            bottom = jnp.where(columns[:half] < half, -bottom, bottom)
            full = jnp.concatenate([top, bottom], axis=0)
            norm = jnp.sqrt(jnp.sum(full * full, axis=(0, 1), keepdims=True) + 1e-06)
            iterates.append(full / norm)
        whiteners = [None] * FREQ
        for at in range(ITERS):
            for f in range(FREQ):
                both = iterates[f] if at == 0 else exact(whiteners[f], iterates[f])
                fix = lift - 0.5 * both
                if at < ITERS - 1:
                    iterates[f] = exact(iterates[f], fix)
                whiteners[f] = fix if at == 0 else exact(fix, whiteners[f])
        for f in range(FREQ):
            straight = jnp.where(rows < half, whiteners[f], -whiteners[f])
            crossed = pltpu.roll(whiteners[f], half, 0)
            shape = (width, out_cols)
            value = jnp.dot(
                straight.astype(jnp.bfloat16), spot(shape, 2 * f * RANK, 0, RANK),
                preferred_element_type=jnp.float32)
            value += jnp.dot(
                crossed.astype(jnp.bfloat16), spot(shape, (2 * f + 1) * RANK, 0, RANK),
                preferred_element_type=jnp.float32)
            projector[:, f * width : (f + 1) * width] = value.T.astype(jnp.bfloat16)

    modes_ref[...] = lax.dot_general(
        projector[...], z_ref[...], (((1,), (1,)), ((), ())),
        preferred_element_type=jnp.float32).astype(modes_ref.dtype)


def project_call(top, weighted):
    rows, cols = weighted.shape
    out_cols = FREQ * 2 * RANK
    tile = 1024
    return pl.pallas_call(
        project_kernel,
        grid=(rows // tile,),
        out_shape=jax.ShapeDtypeStruct((out_cols, rows), jnp.bfloat16),
        in_specs=[
            pl.BlockSpec(top.shape, lambda i: (0, 0)),
            pl.BlockSpec((tile, cols), lambda i: (i, 0)),
        ],
        out_specs=pl.BlockSpec((out_cols, tile), lambda i: (0, i)),
        scratch_shapes=[pltpu.VMEM((out_cols, cols), jnp.bfloat16)],
        compiler_params=pltpu.CompilerParams(
            vmem_limit_bytes=32 << 20, dimension_semantics=("arbitrary",)),
        name="project",
    )(top, weighted)


def local(n_row, n_sub, spectra, mass_blocks, offsets, counts):
    rows, cols = spectra.shape[1:]
    size = mass_blocks.shape[3]
    weighted, total = weigh_call(
        n_row, n_sub, counts, offsets[0].T,
        spectra[0].reshape(rows // size, size, cols), mass_blocks[0])
    width = cols // FREQ
    modes = project_call(
        total.reshape(FREQ * width // 2, width), weighted.reshape(rows, cols))
    return modes.T[None]


def solution(mesh):
    return jax.shard_map(
        functools.partial(local, mesh.shape["row"], mesh.shape["sub"]),
        mesh=mesh,
        in_specs=(
            P("sub", "row", None),
            P("sub", "row", None, None, None),
            P("sub", "row", None),
            P("sub"),
        ),
        out_specs=P("sub", "row", None),
        check_vma=False,
    )
```

```python
import functools

import jax
import jax.numpy as jnp
from jax import lax
from jax.experimental import pallas as pl
from jax.experimental.pallas import tpu as pltpu
from jax.sharding import PartitionSpec as P

RANK = 48
FREQ = 2
ITERS = 5
HB = 16
GROUP = 4
MESH = pl.DeviceIdType.MESH


def peer_copy(src, dst, send, recv, axis, index):
    return pltpu.make_async_remote_copy(
        src_ref=src, dst_ref=dst, send_sem=send, recv_sem=recv,
        device_id={axis: index}, device_id_type=MESH,
    )


def masked(value, rows, first, count):
    live = jnp.clip(count - first, 0, value.shape[0]).astype(jnp.float32)
    bound = jnp.full(value.shape, live, jnp.float32).astype(jnp.bfloat16)
    return jnp.where(rows < bound, value, jnp.zeros((), value.dtype))


def realify(part):
    width = part.shape[0]
    half = width // 2
    swapped = pltpu.roll(pltpu.roll(part, half, 0), half, 1)
    low_row = lax.broadcasted_iota(jnp.int32, part.shape, 0) < half
    low_col = lax.broadcasted_iota(jnp.int32, part.shape, 1) < half
    return swapped + jnp.where(low_row == low_col, part, -part)


def place(step, steps):
    edge, pair = HB // GROUP, HB // GROUP // 2
    inside = steps - 2 * edge
    late = step - inside
    turn = late // pair
    within = late % pair
    outer = jnp.where(
        turn == 0, steps - edge + within,
        jnp.where(turn == 1, pair + within, jnp.where(turn == 2, steps - pair + within, within)))
    return jnp.where(step < inside, step + edge, outer)


def weigh_kernel(
    n_row, n_sub, count_ref, offsets_ref, spectra_ref, mass_ref,
    weighted_ref, total_ref,
    own, low_near, low_far, high_near, high_far, rows_in, latest, gram, packed, landed, subs, gathered,
    load_sem, fill_sem, halo_send, halo_recv,
    first_send, first_recv, second_send, second_recv, third_send, third_recv,
):
    step = pl.program_id(0)
    steps = pl.num_programs(0)
    row = lax.axis_index("row")
    sub = lax.axis_index("sub")
    blocks, size, cols = own.shape
    reach = HB
    slots = mass_ref.shape[1]
    near = reach // 2
    pair = near // GROUP
    group = place(step, steps)
    count = count_ref[0]
    base = row * blocks
    after = lax.rem(row + 1, n_row)
    before = lax.rem(row + n_row - 1, n_row)

    def halo(src_at, dst, dst_at, sem, peer):
        return peer_copy(
            spectra_ref.at[pl.ds(src_at, near)], dst.at[pl.ds(dst_at, near)],
            halo_send.at[sem], halo_recv.at[sem], "row", peer)

    to_next = [halo(blocks - near, low_near, 0, 0, after),
               halo(blocks - reach, low_far, 0, 1, after)]
    to_prev = [halo(0, high_near, 2 * reach, 2, before),
               halo(near, high_far, 2 * reach, 3, before)]
    most = 2 * reach
    part = reach + near
    fills = [
        pltpu.make_async_copy(own.at[pl.ds(at, length)], buffer.at[pl.ds(to, length)],
                              fill_sem.at[sem])
        for sem, (at, length, buffer, to) in enumerate((
            (blocks - most, most, high_near, 0),
            (0, most, low_near, near),
            (blocks - part, part, high_far, 0),
            (0, part, low_far, reach),
        ))
    ]

    @pl.when(step == 0)
    def _():
        barrier = pltpu.get_barrier_semaphore()
        for j in range(1, n_row):
            pl.semaphore_signal(barrier, inc=1, device_id={"row": lax.rem(row + j, n_row)},
                                device_id_type=MESH)
        for j in range(1, n_sub):
            pl.semaphore_signal(barrier, inc=1, device_id={"sub": lax.rem(sub + j, n_sub)},
                                device_id_type=MESH)
        load = pltpu.make_async_copy(spectra_ref, own, load_sem)
        load.start()
        gram[...] = jnp.zeros_like(gram)
        latest[...] = jnp.zeros_like(latest)
        rows_in[...] = lax.broadcasted_iota(jnp.int32, (size, cols), 0).astype(
            jnp.float32).astype(jnp.bfloat16)

        @pl.when(row == 0)
        def _():
            low_near[pl.ds(0, near)] = jnp.zeros((near, size, cols), low_near.dtype)
            low_far[pl.ds(0, near)] = jnp.zeros((near, size, cols), low_far.dtype)

        @pl.when(row == n_row - 1)
        def _():
            high_near[pl.ds(most, near)] = jnp.zeros((near, size, cols), high_near.dtype)
            high_far[pl.ds(most, near)] = jnp.zeros((near, size, cols), high_far.dtype)

        pl.semaphore_wait(barrier, n_row + n_sub - 2)

        for at in range(2):
            @pl.when(row < n_row - 1)
            def _():
                to_next[at].start()

            @pl.when(row > 0)
            def _():
                to_prev[at].start()

        load.wait()

        def clear(b, carry):
            own[b] = masked(own[b], rows_in[...], (base + b) * size, count)
            return carry

        lax.fori_loop(0, blocks, clear, 0)
        for fill in fills:
            fill.start()

    def clear_halo(buffer, start, first_block, other=None, other_start=0):
        def body(b, carry):
            value = masked(buffer[start + b], rows_in[...], (first_block + b) * size, count)
            buffer[start + b] = value
            if other is not None:
                other[other_start + b] = value
            return carry
        lax.fori_loop(0, near, body, 0)

    inside = steps - 4 * pair

    @pl.when(step == inside)
    def _():
        @pl.when(row < n_row - 1)
        def _():
            to_prev[0].wait_recv()
        fills[0].wait()
        clear_halo(high_near, most, base + blocks, high_far, part)

    @pl.when(step == inside + pair)
    def _():
        @pl.when(row > 0)
        def _():
            to_next[0].wait_recv()
        fills[1].wait()
        clear_halo(low_near, 0, base - near, low_far, near)

    @pl.when(step == inside + 2 * pair)
    def _():
        @pl.when(row < n_row - 1)
        def _():
            to_prev[1].wait_recv()
        fills[2].wait()
        clear_halo(high_far, most, base + blocks + near)

    @pl.when(step == inside + 3 * pair)
    def _():
        @pl.when(row > 0)
        def _():
            to_next[1].wait_recv()
        fills[3].wait()
        clear_halo(low_far, 0, base - reach)

    def add_gram():
        z = latest[...]
        gram[...] += lax.dot_general(z, z, (((0,), (0,)), ((), ())),
                                     preferred_element_type=jnp.float32)

    def weigh(buffer, shift):
        fresh = []
        for r in range(GROUP):
            at = group * GROUP + r
            summed = None
            for k in range(0, slots, 2):
                ks = range(k, min(k + 2, slots))
                picks = [buffer[at + shift + offsets_ref[k, 0, at]] for k in ks]
                product = jnp.dot(
                    jnp.concatenate([mass_ref[r, k] for k in ks], axis=1),
                    jnp.concatenate(picks, axis=0), preferred_element_type=jnp.float32)
                summed = product if summed is None else summed + product
            value = masked(summed.astype(weighted_ref.dtype), rows_in[...],
                           (base + at) * size, count)
            weighted_ref[r] = value
            fresh.append(value)
        add_gram()
        latest[...] = jnp.concatenate(fresh, axis=0)

    for least, buffer, shift in (
        (0, own, 0),
        (1, high_near, most - blocks),
        (2, low_near, near),
        (3, high_far, part - blocks),
        (4, low_far, reach),
    ):
        first = 0 if least == 0 else inside + (least - 1) * pair
        last = inside + least * pair

        @pl.when(jnp.logical_and(step >= first, step < last))
        def _():
            weigh(buffer, shift)

    @pl.when(step == steps - 1)
    def _():
        add_gram()
        width = cols // FREQ
        depth = packed.shape[1]
        for f in range(FREQ):
            cut = slice(f * width, (f + 1) * width)
            top = realify(gram[cut, cut])[: width // 2]
            pieces = (width // 2) // depth
            packed[f * pieces : (f + 1) * pieces] = top.reshape(pieces, depth, width)

        def spread(n, axis, me, src, slot_of, send, recv):
            copies = []
            for j in range(1, n):
                peer = lax.rem(me + j, n)
                copy = peer_copy(src(peer), slot_of(me), send.at[j], recv.at[j], axis, peer)
                copy.start()
                copies.append(copy)
            for j in range(1, n):
                peer = lax.rem(me + n - j, n)
                peer_copy(src(peer), slot_of(peer), send.at[j], recv.at[j], axis, peer).wait_recv()
            return copies

        first = spread(n_row, "row", row, lambda p: packed.at[p], lambda s: landed.at[s],
                       first_send, first_recv)
        landed[row] = packed[row]
        partial = landed[0]
        for j in range(1, n_row):
            partial = partial + landed[j]
        subs[sub] = partial
        second = spread(n_sub, "sub", sub, lambda p: subs.at[sub], lambda s: subs.at[s],
                        second_send, second_recv)
        whole = subs[0]
        for j in range(1, n_sub):
            whole = whole + subs[j]
        gathered[row] = whole
        third = spread(n_row, "row", row, lambda p: gathered.at[row], lambda s: gathered.at[s],
                       third_send, third_recv)
        total_ref[...] = gathered[...]

        for at in range(2):
            @pl.when(row < n_row - 1)
            def _():
                to_next[at].wait_send()

            @pl.when(row > 0)
            def _():
                to_prev[at].wait_send()

        for copy in first + second + third:
            copy.wait_send()


def weigh_call(n_row, n_sub, counts, offsets, spectra, mass_blocks):
    blocks, size, cols = spectra.shape
    slots = mass_blocks.shape[1]
    steps = blocks // GROUP
    window = 2 * HB + HB // 2
    width = cols // FREQ
    depth = FREQ * (width // 2) // n_row
    dma = pltpu.SemaphoreType.DMA

    return pl.pallas_call(
        functools.partial(weigh_kernel, n_row, n_sub),
        grid=(steps,),
        out_shape=(
            jax.ShapeDtypeStruct((blocks, size, cols), jnp.bfloat16),
            jax.ShapeDtypeStruct((n_row, depth, width), jnp.float32),
        ),
        in_specs=[
            pl.BlockSpec(memory_space=pltpu.SMEM),
            pl.BlockSpec(memory_space=pltpu.SMEM),
            pl.BlockSpec(memory_space=pltpu.HBM),
            pl.BlockSpec((GROUP, slots, size, size), lambda i: (place(i, steps), 0, 0, 0)),
        ],
        out_specs=(
            pl.BlockSpec((GROUP, size, cols), lambda i: (place(i, steps), 0, 0)),
            pl.BlockSpec(memory_space=pltpu.VMEM),
        ),
        scratch_shapes=[
            pltpu.VMEM((blocks, size, cols), jnp.bfloat16),
            pltpu.VMEM((window, size, cols), jnp.bfloat16),
            pltpu.VMEM((window, size, cols), jnp.bfloat16),
            pltpu.VMEM((window, size, cols), jnp.bfloat16),
            pltpu.VMEM((window, size, cols), jnp.bfloat16),
            pltpu.VMEM((size, cols), jnp.bfloat16),
            pltpu.VMEM((GROUP * size, cols), jnp.bfloat16),
            pltpu.VMEM((cols, cols), jnp.float32),
            pltpu.VMEM((n_row, depth, width), jnp.float32),
            pltpu.VMEM((n_row, depth, width), jnp.float32),
            pltpu.VMEM((n_sub, depth, width), jnp.float32),
            pltpu.VMEM((n_row, depth, width), jnp.float32),
            dma, dma((4,)), dma((4,)), dma((4,)),
            dma((n_row,)), dma((n_row,)),
            dma((n_sub,)), dma((n_sub,)),
            dma((n_row,)), dma((n_row,)),
        ],
        compiler_params=pltpu.CompilerParams(
            collective_id=0, has_side_effects=True, vmem_limit_bytes=60 << 20,
            dimension_semantics=("arbitrary",),
        ),
        name="weigh",
    )(counts, offsets, spectra, mass_blocks)


def spot(shape, shift, least, most):
    source = lax.broadcasted_iota(jnp.int32, shape, 0)
    target = lax.broadcasted_iota(jnp.int32, shape, 1)
    hit = (target == source + shift) & (source >= least) & (source < most)
    return jnp.where(hit, 1.0, 0.0).astype(jnp.bfloat16)


def halves(value):
    head = value.astype(jnp.bfloat16)
    return head, (value - head.astype(jnp.float32)).astype(jnp.bfloat16)


def exact(first, second):
    a, a_rest = halves(first)
    b, b_rest = halves(second)
    return jnp.dot(
        jnp.concatenate([a, a, a_rest], axis=1), jnp.concatenate([b, b_rest, b], axis=0),
        preferred_element_type=jnp.float32)


def project_kernel(top_ref, z_ref, modes_ref, projector):
    @pl.when(pl.program_id(0) == 0)
    def _():
        width = top_ref.shape[1]
        half = width // 2
        out_cols = projector.shape[0]
        rows = lax.broadcasted_iota(jnp.int32, (width, width), 0)
        columns = lax.broadcasted_iota(jnp.int32, (width, width), 1)
        lift = jnp.where(rows == columns, 1.5, 0.0)
        iterates = []
        for f in range(FREQ):
            top = top_ref[f * half : (f + 1) * half]
            bottom = pltpu.roll(top, half, 1)
            bottom = jnp.where(columns[:half] < half, -bottom, bottom)
            full = jnp.concatenate([top, bottom], axis=0)
            norm = jnp.sqrt(jnp.sum(full * full, axis=(0, 1), keepdims=True) + 1e-06)
            iterates.append(full / norm)
        whiteners = [None] * FREQ
        for at in range(ITERS):
            for f in range(FREQ):
                both = iterates[f] if at == 0 else exact(whiteners[f], iterates[f])
                fix = lift - 0.5 * both
                if at < ITERS - 1:
                    iterates[f] = exact(iterates[f], fix)
                whiteners[f] = fix if at == 0 else exact(fix, whiteners[f])
        for f in range(FREQ):
            straight = jnp.where(rows < half, whiteners[f], -whiteners[f])
            crossed = pltpu.roll(whiteners[f], half, 0)
            shape = (width, out_cols)
            value = jnp.dot(
                straight.astype(jnp.bfloat16), spot(shape, 2 * f * RANK, 0, RANK),
                preferred_element_type=jnp.float32)
            value += jnp.dot(
                crossed.astype(jnp.bfloat16), spot(shape, (2 * f + 1) * RANK, 0, RANK),
                preferred_element_type=jnp.float32)
            projector[:, f * width : (f + 1) * width] = value.T.astype(jnp.bfloat16)

    modes_ref[...] = lax.dot_general(
        projector[...], z_ref[...], (((1,), (1,)), ((), ())),
        preferred_element_type=jnp.float32).astype(modes_ref.dtype)


def project_call(top, weighted):
    rows, cols = weighted.shape
    out_cols = FREQ * 2 * RANK
    tile = 1024
    return pl.pallas_call(
        project_kernel,
        grid=(rows // tile,),
        out_shape=jax.ShapeDtypeStruct((out_cols, rows), jnp.bfloat16),
        in_specs=[
            pl.BlockSpec(top.shape, lambda i: (0, 0)),
            pl.BlockSpec((tile, cols), lambda i: (i, 0)),
        ],
        out_specs=pl.BlockSpec((out_cols, tile), lambda i: (0, i)),
        scratch_shapes=[pltpu.VMEM((out_cols, cols), jnp.bfloat16)],
        compiler_params=pltpu.CompilerParams(
            vmem_limit_bytes=60 << 20, dimension_semantics=("arbitrary",)),
        name="project",
    )(top, weighted)


def local(n_row, n_sub, spectra, mass_blocks, offsets, counts):
    rows, cols = spectra.shape[1:]
    size = mass_blocks.shape[3]
    weighted, total = weigh_call(
        n_row, n_sub, counts, offsets.transpose(2, 0, 1),
        spectra[0].reshape(rows // size, size, cols), mass_blocks[0])
    width = cols // FREQ
    modes = project_call(
        total.reshape(FREQ * width // 2, width), weighted.reshape(rows, cols))
    return modes.T[None]


def solution(mesh):
    return jax.shard_map(
        functools.partial(local, mesh.shape["row"], mesh.shape["sub"]),
        mesh=mesh,
        in_specs=(
            P("sub", "row", None),
            P("sub", "row", None, None, None),
            P("sub", "row", None),
            P("sub"),
        ),
        out_specs=P("sub", "row", None),
        check_vma=False,
    )
```

```python
import functools

import jax
import jax.numpy as jnp
from jax import lax
from jax.experimental import pallas as pl
from jax.experimental.pallas import tpu as pltpu
from jax.sharding import PartitionSpec as P

RANK = 48
FREQ = 2
ITERS = 5
HB = 16
GROUP = 4
MESH = pl.DeviceIdType.MESH


def peer_copy(src, dst, send, recv, axis, index):
    return pltpu.make_async_remote_copy(
        src_ref=src, dst_ref=dst, send_sem=send, recv_sem=recv,
        device_id={axis: index}, device_id_type=MESH,
    )


def masked(value, rows, first, count):
    live = jnp.clip(count - first, 0, value.shape[0]).astype(jnp.float32)
    bound = jnp.full(value.shape, live, jnp.float32).astype(jnp.bfloat16)
    return jnp.where(rows < bound, value, jnp.zeros((), value.dtype))


def realify(part):
    width = part.shape[0]
    half = width // 2
    swapped = pltpu.roll(pltpu.roll(part, half, 0), half, 1)
    low_row = lax.broadcasted_iota(jnp.int32, part.shape, 0) < half
    low_col = lax.broadcasted_iota(jnp.int32, part.shape, 1) < half
    return swapped + jnp.where(low_row == low_col, part, -part)


def place(step, steps):
    edge, pair = HB // GROUP, HB // GROUP // 2
    inside = steps - 2 * edge
    late = step - inside
    turn = late // pair
    within = late % pair
    outer = jnp.where(
        turn == 0, steps - edge + within,
        jnp.where(turn == 1, pair + within, jnp.where(turn == 2, steps - pair + within, within)))
    return jnp.where(step < inside, step + edge, outer)


def weigh_kernel(
    n_row, n_sub, count_ref, offsets_ref, spectra_ref, mass_ref,
    weighted_ref, total_ref,
    own, low_near, low_far, high_near, high_far, rows_in, relay, latest, gram, packed, landed, subs, gathered,
    load_sem, relay_send, relay_recv, fill_sem, halo_send, halo_recv,
    first_send, first_recv, second_send, second_recv, third_send, third_recv,
):
    step = pl.program_id(0)
    steps = pl.num_programs(0)
    row = lax.axis_index("row")
    sub = lax.axis_index("sub")
    blocks, size, cols = own.shape
    reach = HB
    slots = mass_ref.shape[1]
    near = reach // 2
    pair = near // GROUP
    group = place(step, steps)
    count = count_ref[0]
    base = row * blocks
    after = lax.rem(row + 1, n_row)
    before = lax.rem(row + n_row - 1, n_row)

    def halo(src_at, dst, dst_at, sem, peer):
        return peer_copy(
            spectra_ref.at[pl.ds(src_at, near)], dst.at[pl.ds(dst_at, near)],
            halo_send.at[sem], halo_recv.at[sem], "row", peer)

    to_next = [halo(blocks - near, low_near, 0, 0, after),
               halo(blocks - reach, low_far, 0, 1, after)]
    to_prev = [halo(0, high_near, 2 * reach, 2, before),
               halo(near, high_far, 2 * reach, 3, before)]
    most = 2 * reach
    part = reach + near
    relays = [(3, 7, 4), (4, 0, 3)] if n_row == 8 else []
    direct = [row < n_row - 1, row > 0]
    for source, via, goal in relays:
        side = 0 if goal > source else 1
        direct[side] = jnp.logical_and(direct[side], row != source)
    sends = [(to_next[0], row < n_row - 1), (to_prev[0], row > 0)]
    onward = []
    for source, via, goal in relays:
        at = blocks - reach if goal > source else near
        into = peer_copy(spectra_ref.at[pl.ds(at, near)], relay, relay_send, relay_recv, "row", via)
        sends.append((into, row == source))
        far, to, sem = (low_far, 0, 1) if goal > source else (high_far, most, 3)
        onward.append((via, into, peer_copy(
            relay, far.at[pl.ds(to, near)], halo_send.at[sem], halo_recv.at[sem], "row", goal)))
    sends += [(to_next[1], direct[0]), (to_prev[1], direct[1])]
    fills = [
        pltpu.make_async_copy(own.at[pl.ds(at, length)], buffer.at[pl.ds(to, length)],
                              fill_sem.at[sem])
        for sem, (at, length, buffer, to) in enumerate((
            (blocks - most, most, high_near, 0),
            (0, most, low_near, near),
            (blocks - part, part, high_far, 0),
            (0, part, low_far, reach),
        ))
    ]

    @pl.when(step == 0)
    def _():
        barrier = pltpu.get_barrier_semaphore()
        for j in range(1, n_row):
            pl.semaphore_signal(barrier, inc=1, device_id={"row": lax.rem(row + j, n_row)},
                                device_id_type=MESH)
        for j in range(1, n_sub):
            pl.semaphore_signal(barrier, inc=1, device_id={"sub": lax.rem(sub + j, n_sub)},
                                device_id_type=MESH)
        load = pltpu.make_async_copy(spectra_ref, own, load_sem)
        load.start()
        gram[...] = jnp.zeros_like(gram)
        latest[...] = jnp.zeros_like(latest)
        rows_in[...] = lax.broadcasted_iota(jnp.int32, (size, cols), 0).astype(
            jnp.float32).astype(jnp.bfloat16)

        @pl.when(row == 0)
        def _():
            low_near[pl.ds(0, near)] = jnp.zeros((near, size, cols), low_near.dtype)
            low_far[pl.ds(0, near)] = jnp.zeros((near, size, cols), low_far.dtype)

        @pl.when(row == n_row - 1)
        def _():
            high_near[pl.ds(most, near)] = jnp.zeros((near, size, cols), high_near.dtype)
            high_far[pl.ds(most, near)] = jnp.zeros((near, size, cols), high_far.dtype)

        pl.semaphore_wait(barrier, n_row + n_sub - 2)

        for copy, mine in sends:
            @pl.when(mine)
            def _():
                copy.start()

        load.wait()

        def clear(b, carry):
            own[b] = masked(own[b], rows_in[...], (base + b) * size, count)
            return carry

        lax.fori_loop(0, blocks, clear, 0)
        for fill in fills:
            fill.start()

    def clear_halo(buffer, start, first_block, other=None, other_start=0):
        def body(b, carry):
            value = masked(buffer[start + b], rows_in[...], (first_block + b) * size, count)
            buffer[start + b] = value
            if other is not None:
                other[other_start + b] = value
            return carry
        lax.fori_loop(0, near, body, 0)

    inside = steps - 4 * pair

    @pl.when(step == inside - 3)
    def _():
        for via, into, forward in onward:
            @pl.when(row == via)
            def _():
                into.wait_recv()
                forward.start()

    @pl.when(step == inside)
    def _():
        @pl.when(row < n_row - 1)
        def _():
            to_prev[0].wait_recv()
        fills[0].wait()
        clear_halo(high_near, most, base + blocks, high_far, part)

    @pl.when(step == inside + pair)
    def _():
        @pl.when(row > 0)
        def _():
            to_next[0].wait_recv()
        fills[1].wait()
        clear_halo(low_near, 0, base - near, low_far, near)

    @pl.when(step == inside + 2 * pair)
    def _():
        @pl.when(row < n_row - 1)
        def _():
            to_prev[1].wait_recv()
        fills[2].wait()
        clear_halo(high_far, most, base + blocks + near)

    @pl.when(step == inside + 3 * pair)
    def _():
        @pl.when(row > 0)
        def _():
            to_next[1].wait_recv()
        fills[3].wait()
        clear_halo(low_far, 0, base - reach)

    def add_gram():
        z = latest[...]
        gram[...] += lax.dot_general(z, z, (((0,), (0,)), ((), ())),
                                     preferred_element_type=jnp.float32)

    def weigh(buffer, shift):
        fresh = []
        for r in range(GROUP):
            at = group * GROUP + r
            summed = None
            for k in range(0, slots, 2):
                ks = range(k, min(k + 2, slots))
                picks = [buffer[at + shift + offsets_ref[k, 0, at]] for k in ks]
                product = jnp.dot(
                    jnp.concatenate([mass_ref[r, k] for k in ks], axis=1),
                    jnp.concatenate(picks, axis=0), preferred_element_type=jnp.float32)
                summed = product if summed is None else summed + product
            value = masked(summed.astype(weighted_ref.dtype), rows_in[...],
                           (base + at) * size, count)
            weighted_ref[r] = value
            fresh.append(value)
        add_gram()
        latest[...] = jnp.concatenate(fresh, axis=0)

    for least, buffer, shift in (
        (0, own, 0),
        (1, high_near, most - blocks),
        (2, low_near, near),
        (3, high_far, part - blocks),
        (4, low_far, reach),
    ):
        first = 0 if least == 0 else inside + (least - 1) * pair
        last = inside + least * pair

        @pl.when(jnp.logical_and(step >= first, step < last))
        def _():
            weigh(buffer, shift)

    @pl.when(step == steps - 1)
    def _():
        add_gram()
        width = cols // FREQ
        depth = packed.shape[1]
        for f in range(FREQ):
            cut = slice(f * width, (f + 1) * width)
            top = realify(gram[cut, cut])[: width // 2]
            pieces = (width // 2) // depth
            packed[f * pieces : (f + 1) * pieces] = top.reshape(pieces, depth, width)

        def spread(n, axis, me, src, slot_of, send, recv):
            copies = []
            for j in range(1, n):
                peer = lax.rem(me + j, n)
                copy = peer_copy(src(peer), slot_of(me), send.at[j], recv.at[j], axis, peer)
                copy.start()
                copies.append(copy)
            for j in range(1, n):
                peer = lax.rem(me + n - j, n)
                peer_copy(src(peer), slot_of(peer), send.at[j], recv.at[j], axis, peer).wait_recv()
            return copies

        first = spread(n_row, "row", row, lambda p: packed.at[p], lambda s: landed.at[s],
                       first_send, first_recv)
        landed[row] = packed[row]
        partial = landed[0]
        for j in range(1, n_row):
            partial = partial + landed[j]
        subs[sub] = partial
        second = spread(n_sub, "sub", sub, lambda p: subs.at[sub], lambda s: subs.at[s],
                        second_send, second_recv)
        whole = subs[0]
        for j in range(1, n_sub):
            whole = whole + subs[j]
        gathered[row] = whole
        third = spread(n_row, "row", row, lambda p: gathered.at[row], lambda s: gathered.at[s],
                       third_send, third_recv)
        total_ref[...] = gathered[...]

        for copy, mine in sends + [(forward, row == via) for via, into, forward in onward]:
            @pl.when(mine)
            def _():
                copy.wait_send()

        for copy in first + second + third:
            copy.wait_send()


def weigh_call(n_row, n_sub, counts, offsets, spectra, mass_blocks):
    blocks, size, cols = spectra.shape
    slots = mass_blocks.shape[1]
    steps = blocks // GROUP
    window = 2 * HB + HB // 2
    width = cols // FREQ
    depth = FREQ * (width // 2) // n_row
    dma = pltpu.SemaphoreType.DMA

    return pl.pallas_call(
        functools.partial(weigh_kernel, n_row, n_sub),
        grid=(steps,),
        out_shape=(
            jax.ShapeDtypeStruct((blocks, size, cols), jnp.bfloat16),
            jax.ShapeDtypeStruct((n_row, depth, width), jnp.float32),
        ),
        in_specs=[
            pl.BlockSpec(memory_space=pltpu.SMEM),
            pl.BlockSpec(memory_space=pltpu.SMEM),
            pl.BlockSpec(memory_space=pltpu.HBM),
            pl.BlockSpec((GROUP, slots, size, size), lambda i: (place(i, steps), 0, 0, 0)),
        ],
        out_specs=(
            pl.BlockSpec((GROUP, size, cols), lambda i: (place(i, steps), 0, 0)),
            pl.BlockSpec(memory_space=pltpu.VMEM),
        ),
        scratch_shapes=[
            pltpu.VMEM((blocks, size, cols), jnp.bfloat16),
            pltpu.VMEM((window, size, cols), jnp.bfloat16),
            pltpu.VMEM((window, size, cols), jnp.bfloat16),
            pltpu.VMEM((window, size, cols), jnp.bfloat16),
            pltpu.VMEM((window, size, cols), jnp.bfloat16),
            pltpu.VMEM((size, cols), jnp.bfloat16),
            pltpu.VMEM((HB // 2, size, cols), jnp.bfloat16),
            pltpu.VMEM((GROUP * size, cols), jnp.bfloat16),
            pltpu.VMEM((cols, cols), jnp.float32),
            pltpu.VMEM((n_row, depth, width), jnp.float32),
            pltpu.VMEM((n_row, depth, width), jnp.float32),
            pltpu.VMEM((n_sub, depth, width), jnp.float32),
            pltpu.VMEM((n_row, depth, width), jnp.float32),
            dma, dma, dma, dma((4,)), dma((4,)), dma((4,)),
            dma((n_row,)), dma((n_row,)),
            dma((n_sub,)), dma((n_sub,)),
            dma((n_row,)), dma((n_row,)),
        ],
        compiler_params=pltpu.CompilerParams(
            collective_id=0, has_side_effects=True, vmem_limit_bytes=60 << 20,
            dimension_semantics=("arbitrary",),
        ),
        name="weigh",
    )(counts, offsets, spectra, mass_blocks)


def spot(shape, shift, least, most):
    source = lax.broadcasted_iota(jnp.int32, shape, 0)
    target = lax.broadcasted_iota(jnp.int32, shape, 1)
    hit = (target == source + shift) & (source >= least) & (source < most)
    return jnp.where(hit, 1.0, 0.0).astype(jnp.bfloat16)


def halves(value):
    head = value.astype(jnp.bfloat16)
    return head, (value - head.astype(jnp.float32)).astype(jnp.bfloat16)


def exact(first, second):
    a, a_rest = halves(first)
    b, b_rest = halves(second)
    return jnp.dot(
        jnp.concatenate([a, a, a_rest], axis=1), jnp.concatenate([b, b_rest, b], axis=0),
        preferred_element_type=jnp.float32)


def project_kernel(top_ref, weighted_ref, modes_ref, projector, z_ref, load_sem):
    @pl.when(pl.program_id(0) == 0)
    def _():
        load = pltpu.make_async_copy(weighted_ref, z_ref, load_sem)
        load.start()
        width = top_ref.shape[1]
        half = width // 2
        out_cols = projector.shape[0]
        rows = lax.broadcasted_iota(jnp.int32, (width, width), 0)
        columns = lax.broadcasted_iota(jnp.int32, (width, width), 1)
        lift = jnp.where(rows == columns, 1.5, 0.0)
        iterates = []
        for f in range(FREQ):
            top = top_ref[f * half : (f + 1) * half]
            bottom = pltpu.roll(top, half, 1)
            bottom = jnp.where(columns[:half] < half, -bottom, bottom)
            full = jnp.concatenate([top, bottom], axis=0)
            norm = jnp.sqrt(jnp.sum(full * full, axis=(0, 1), keepdims=True) + 1e-06)
            iterates.append(full / norm)
        whiteners = [None] * FREQ
        for at in range(ITERS):
            for f in range(FREQ):
                both = iterates[f] if at == 0 else exact(whiteners[f], iterates[f])
                fix = lift - 0.5 * both
                if at < ITERS - 1:
                    iterates[f] = exact(iterates[f], fix)
                whiteners[f] = fix if at == 0 else exact(fix, whiteners[f])
        for f in range(FREQ):
            straight = jnp.where(rows < half, whiteners[f], -whiteners[f])
            crossed = pltpu.roll(whiteners[f], half, 0)
            shape = (width, out_cols)
            value = jnp.dot(
                straight.astype(jnp.bfloat16), spot(shape, 2 * f * RANK, 0, RANK),
                preferred_element_type=jnp.float32)
            value += jnp.dot(
                crossed.astype(jnp.bfloat16), spot(shape, (2 * f + 1) * RANK, 0, RANK),
                preferred_element_type=jnp.float32)
            projector[:, f * width : (f + 1) * width] = value.T.astype(jnp.bfloat16)
        load.wait()

    tile = modes_ref.shape[1]
    at = pl.multiple_of(pl.program_id(0) * tile, tile)

    modes_ref[...] = lax.dot_general(
        projector[...], z_ref[pl.ds(at, tile)], (((1,), (1,)), ((), ())),
        preferred_element_type=jnp.float32).astype(modes_ref.dtype)


def project_call(top, weighted):
    rows, cols = weighted.shape
    out_cols = FREQ * 2 * RANK
    tile = 1024
    return pl.pallas_call(
        project_kernel,
        grid=(rows // tile,),
        out_shape=jax.ShapeDtypeStruct((out_cols, rows), jnp.bfloat16),
        in_specs=[
            pl.BlockSpec(top.shape, lambda i: (0, 0)),
            pl.BlockSpec(memory_space=pl.ANY),
        ],
        out_specs=pl.BlockSpec((out_cols, tile), lambda i: (0, i)),
        scratch_shapes=[
            pltpu.VMEM((out_cols, cols), jnp.bfloat16),
            pltpu.VMEM((rows, cols), jnp.bfloat16),
            pltpu.SemaphoreType.DMA,
        ],
        compiler_params=pltpu.CompilerParams(
            vmem_limit_bytes=60 << 20, dimension_semantics=("arbitrary",)),
        name="project",
    )(top, weighted)


def local(n_row, n_sub, spectra, mass_blocks, offsets, counts):
    rows, cols = spectra.shape[1:]
    size = mass_blocks.shape[3]
    weighted, total = weigh_call(
        n_row, n_sub, counts, offsets.transpose(2, 0, 1),
        spectra[0].reshape(rows // size, size, cols), mass_blocks[0])
    width = cols // FREQ
    modes = project_call(
        total.reshape(FREQ * width // 2, width), weighted.reshape(rows, cols))
    return modes.T[None]


def solution(mesh):
    return jax.shard_map(
        functools.partial(local, mesh.shape["row"], mesh.shape["sub"]),
        mesh=mesh,
        in_specs=(
            P("sub", "row", None),
            P("sub", "row", None, None, None),
            P("sub", "row", None),
            P("sub"),
        ),
        out_specs=P("sub", "row", None),
        check_vma=False,
    )
```

```python
import functools

import jax
import jax.numpy as jnp
from jax import lax
from jax.experimental import pallas as pl
from jax.experimental.pallas import tpu as pltpu
from jax.sharding import PartitionSpec as P

RANK = 48
FREQ = 2
ITERS = 5
HB = 16
GROUP = 4
MESH = pl.DeviceIdType.MESH


def peer_copy(src, dst, send, recv, axis, index):
    return pltpu.make_async_remote_copy(
        src_ref=src, dst_ref=dst, send_sem=send, recv_sem=recv,
        device_id={axis: index}, device_id_type=MESH,
    )


def masked(value, rows, first, count):
    live = jnp.clip(count - first, 0, value.shape[0]).astype(jnp.float32)
    bound = jnp.full(value.shape, live, jnp.float32).astype(jnp.bfloat16)
    return jnp.where(rows < bound, value, jnp.zeros((), value.dtype))


def realify(part):
    width = part.shape[0]
    half = width // 2
    swapped = pltpu.roll(pltpu.roll(part, half, 0), half, 1)
    low_row = lax.broadcasted_iota(jnp.int32, part.shape, 0) < half
    low_col = lax.broadcasted_iota(jnp.int32, part.shape, 1) < half
    return swapped + jnp.where(low_row == low_col, part, -part)


def place(step, steps):
    edge, pair = HB // GROUP, HB // GROUP // 2
    inside = steps - 2 * edge
    late = step - inside
    turn = late // pair
    within = late % pair
    outer = jnp.where(
        turn == 0, steps - edge + within,
        jnp.where(turn == 1, pair + within, jnp.where(turn == 2, steps - pair + within, within)))
    return jnp.where(step < inside, step + edge, outer)


def weigh_kernel(
    n_row, n_sub, count_ref, offsets_ref, spectra_ref, mass_ref,
    weighted_ref, total_ref,
    own, low_near, low_far, high_near, high_far, rows_in, relay, latest, gram, packed, landed, subs, gathered,
    load_sem, relay_send, relay_recv, fill_sem, halo_send, halo_recv,
    first_send, first_recv, second_send, second_recv, third_send, third_recv,
):
    step = pl.program_id(0)
    steps = pl.num_programs(0)
    row = lax.axis_index("row")
    sub = lax.axis_index("sub")
    blocks, size, cols = own.shape
    reach = HB
    slots = mass_ref.shape[1]
    near = reach // 2
    pair = near // GROUP
    group = place(step, steps)
    count = count_ref[0]
    base = row * blocks
    after = lax.rem(row + 1, n_row)
    before = lax.rem(row + n_row - 1, n_row)

    def halo(src_at, dst, dst_at, sem, peer):
        return peer_copy(
            spectra_ref.at[pl.ds(src_at, near)], dst.at[pl.ds(dst_at, near)],
            halo_send.at[sem], halo_recv.at[sem], "row", peer)

    to_next = [halo(blocks - near, low_near, 0, 0, after),
               halo(blocks - reach, low_far, 0, 1, after)]
    to_prev = [halo(0, high_near, 2 * reach, 2, before),
               halo(near, high_far, 2 * reach, 3, before)]
    most = 2 * reach
    part = reach + near
    relays = [(3, 7, 4), (4, 0, 3)] if n_row == 8 else []
    direct = [row < n_row - 1, row > 0]
    for source, via, goal in relays:
        side = 0 if goal > source else 1
        direct[side] = jnp.logical_and(direct[side], row != source)
    sends = [(to_next[0], row < n_row - 1), (to_prev[0], row > 0)]
    onward = []
    for source, via, goal in relays:
        at = blocks - reach if goal > source else near
        into = peer_copy(spectra_ref.at[pl.ds(at, near)], relay, relay_send, relay_recv, "row", via)
        sends.append((into, row == source))
        far, to, sem = (low_far, 0, 1) if goal > source else (high_far, most, 3)
        onward.append((via, into, peer_copy(
            relay, far.at[pl.ds(to, near)], halo_send.at[sem], halo_recv.at[sem], "row", goal)))
    sends += [(to_next[1], direct[0]), (to_prev[1], direct[1])]
    fills = [
        pltpu.make_async_copy(own.at[pl.ds(at, length)], buffer.at[pl.ds(to, length)],
                              fill_sem.at[sem])
        for sem, (at, length, buffer, to) in enumerate((
            (blocks - most, most, high_near, 0),
            (0, most, low_near, near),
            (blocks - part, part, high_far, 0),
            (0, part, low_far, reach),
        ))
    ]

    @pl.when(step == 0)
    def _():
        barrier = pltpu.get_barrier_semaphore()
        for j in range(1, n_row):
            pl.semaphore_signal(barrier, inc=1, device_id={"row": lax.rem(row + j, n_row)},
                                device_id_type=MESH)
        for j in range(1, n_sub):
            pl.semaphore_signal(barrier, inc=1, device_id={"sub": lax.rem(sub + j, n_sub)},
                                device_id_type=MESH)
        load = pltpu.make_async_copy(spectra_ref, own, load_sem)
        load.start()
        gram[...] = jnp.zeros_like(gram)
        latest[...] = jnp.zeros_like(latest)
        rows_in[...] = lax.broadcasted_iota(jnp.int32, (size, cols), 0).astype(
            jnp.float32).astype(jnp.bfloat16)

        @pl.when(row == 0)
        def _():
            low_near[pl.ds(0, near)] = jnp.zeros((near, size, cols), low_near.dtype)
            low_far[pl.ds(0, near)] = jnp.zeros((near, size, cols), low_far.dtype)

        @pl.when(row == n_row - 1)
        def _():
            high_near[pl.ds(most, near)] = jnp.zeros((near, size, cols), high_near.dtype)
            high_far[pl.ds(most, near)] = jnp.zeros((near, size, cols), high_far.dtype)

        pl.semaphore_wait(barrier, n_row + n_sub - 2)

        for copy, mine in sends:
            @pl.when(mine)
            def _():
                copy.start()

        load.wait()

        def clear(b, carry):
            own[b] = masked(own[b], rows_in[...], (base + b) * size, count)
            return carry

        lax.fori_loop(0, blocks, clear, 0)
        for fill in fills:
            fill.start()

    def clear_halo(buffer, start, first_block, other=None, other_start=0):
        def body(b, carry):
            value = masked(buffer[start + b], rows_in[...], (first_block + b) * size, count)
            buffer[start + b] = value
            if other is not None:
                other[other_start + b] = value
            return carry
        lax.fori_loop(0, near, body, 0)

    inside = steps - 4 * pair

    @pl.when(step == inside - 3)
    def _():
        for via, into, forward in onward:
            @pl.when(row == via)
            def _():
                into.wait_recv()
                forward.start()

    @pl.when(step == inside)
    def _():
        @pl.when(row < n_row - 1)
        def _():
            to_prev[0].wait_recv()
        fills[0].wait()
        clear_halo(high_near, most, base + blocks, high_far, part)

    @pl.when(step == inside + pair)
    def _():
        @pl.when(row > 0)
        def _():
            to_next[0].wait_recv()
        fills[1].wait()
        clear_halo(low_near, 0, base - near, low_far, near)

    @pl.when(step == inside + 2 * pair)
    def _():
        @pl.when(row < n_row - 1)
        def _():
            to_prev[1].wait_recv()
        fills[2].wait()
        clear_halo(high_far, most, base + blocks + near)

    @pl.when(step == inside + 3 * pair)
    def _():
        @pl.when(row > 0)
        def _():
            to_next[1].wait_recv()
        fills[3].wait()
        clear_halo(low_far, 0, base - reach)

    def add_gram():
        z = latest[...]
        gram[...] += lax.dot_general(z, z, (((0,), (0,)), ((), ())),
                                     preferred_element_type=jnp.float32)

    def weigh(buffer, shift):
        fresh = []
        for r in range(GROUP):
            at = group * GROUP + r
            summed = None
            for k in range(0, slots, 2):
                ks = range(k, min(k + 2, slots))
                picks = [buffer[at + shift + offsets_ref[k, 0, at]] for k in ks]
                product = jnp.dot(
                    jnp.concatenate([mass_ref[r, k] for k in ks], axis=1),
                    jnp.concatenate(picks, axis=0), preferred_element_type=jnp.float32)
                summed = product if summed is None else summed + product
            value = masked(summed.astype(weighted_ref.dtype), rows_in[...],
                           (base + at) * size, count)
            weighted_ref[r] = value
            fresh.append(value)
        add_gram()
        latest[...] = jnp.concatenate(fresh, axis=0)

    for least, buffer, shift in (
        (0, own, 0),
        (1, high_near, most - blocks),
        (2, low_near, near),
        (3, high_far, part - blocks),
        (4, low_far, reach),
    ):
        first = 0 if least == 0 else inside + (least - 1) * pair
        last = inside + least * pair

        @pl.when(jnp.logical_and(step >= first, step < last))
        def _():
            weigh(buffer, shift)

    @pl.when(step == steps - 1)
    def _():
        add_gram()
        width = cols // FREQ
        depth = packed.shape[1]
        for f in range(FREQ):
            cut = slice(f * width, (f + 1) * width)
            top = realify(gram[cut, cut])[: width // 2]
            pieces = (width // 2) // depth
            packed[f * pieces : (f + 1) * pieces] = top.reshape(pieces, depth, width)

        def spread(n, axis, me, src, slot_of, send, recv):
            copies = []
            for j in range(1, n):
                peer = lax.rem(me + j, n)
                copy = peer_copy(src(peer), slot_of(me), send.at[j], recv.at[j], axis, peer)
                copy.start()
                copies.append(copy)
            for j in range(1, n):
                peer = lax.rem(me + n - j, n)
                peer_copy(src(peer), slot_of(peer), send.at[j], recv.at[j], axis, peer).wait_recv()
            return copies

        first = spread(n_row, "row", row, lambda p: packed.at[p], lambda s: landed.at[s],
                       first_send, first_recv)
        landed[row] = packed[row]
        partial = landed[0]
        for j in range(1, n_row):
            partial = partial + landed[j]
        subs[sub] = partial
        second = spread(n_sub, "sub", sub, lambda p: subs.at[sub], lambda s: subs.at[s],
                        second_send, second_recv)
        whole = subs[0]
        for j in range(1, n_sub):
            whole = whole + subs[j]
        gathered[row] = whole
        third = spread(n_row, "row", row, lambda p: gathered.at[row], lambda s: gathered.at[s],
                       third_send, third_recv)
        total_ref[...] = gathered[...]

        for copy, mine in sends + [(forward, row == via) for via, into, forward in onward]:
            @pl.when(mine)
            def _():
                copy.wait_send()

        for copy in first + second + third:
            copy.wait_send()


def weigh_call(n_row, n_sub, counts, offsets, spectra, mass_blocks):
    blocks, size, cols = spectra.shape
    slots = mass_blocks.shape[1]
    steps = blocks // GROUP
    window = 2 * HB + HB // 2
    width = cols // FREQ
    depth = FREQ * (width // 2) // n_row
    dma = pltpu.SemaphoreType.DMA

    return pl.pallas_call(
        functools.partial(weigh_kernel, n_row, n_sub),
        grid=(steps,),
        out_shape=(
            jax.ShapeDtypeStruct((blocks, size, cols), jnp.bfloat16),
            jax.ShapeDtypeStruct((n_row, depth, width), jnp.float32),
        ),
        in_specs=[
            pl.BlockSpec(memory_space=pltpu.SMEM),
            pl.BlockSpec(memory_space=pltpu.SMEM),
            pl.BlockSpec(memory_space=pltpu.HBM),
            pl.BlockSpec((GROUP, slots, size, size), lambda i: (place(i, steps), 0, 0, 0)),
        ],
        out_specs=(
            pl.BlockSpec((GROUP, size, cols), lambda i: (place(i, steps), 0, 0)),
            pl.BlockSpec(memory_space=pltpu.VMEM),
        ),
        scratch_shapes=[
            pltpu.VMEM((blocks, size, cols), jnp.bfloat16),
            pltpu.VMEM((window, size, cols), jnp.bfloat16),
            pltpu.VMEM((window, size, cols), jnp.bfloat16),
            pltpu.VMEM((window, size, cols), jnp.bfloat16),
            pltpu.VMEM((window, size, cols), jnp.bfloat16),
            pltpu.VMEM((size, cols), jnp.bfloat16),
            pltpu.VMEM((HB // 2, size, cols), jnp.bfloat16),
            pltpu.VMEM((GROUP * size, cols), jnp.bfloat16),
            pltpu.VMEM((cols, cols), jnp.float32),
            pltpu.VMEM((n_row, depth, width), jnp.float32),
            pltpu.VMEM((n_row, depth, width), jnp.float32),
            pltpu.VMEM((n_sub, depth, width), jnp.float32),
            pltpu.VMEM((n_row, depth, width), jnp.float32),
            dma, dma, dma, dma((4,)), dma((4,)), dma((4,)),
            dma((n_row,)), dma((n_row,)),
            dma((n_sub,)), dma((n_sub,)),
            dma((n_row,)), dma((n_row,)),
        ],
        compiler_params=pltpu.CompilerParams(
            collective_id=0, has_side_effects=True, vmem_limit_bytes=60 << 20,
            dimension_semantics=("arbitrary",),
        ),
        name="weigh",
    )(counts, offsets, spectra, mass_blocks)


def spot(shape, shift, least, most):
    source = lax.broadcasted_iota(jnp.int32, shape, 0)
    target = lax.broadcasted_iota(jnp.int32, shape, 1)
    hit = (target == source + shift) & (source >= least) & (source < most)
    return jnp.where(hit, 1.0, 0.0).astype(jnp.bfloat16)


def halves(value):
    head = value.astype(jnp.bfloat16)
    return head, (value - head.astype(jnp.float32)).astype(jnp.bfloat16)


def exact(first, second):
    a, a_rest = halves(first)
    b, b_rest = halves(second)
    return jnp.dot(
        jnp.concatenate([a, a, a_rest], axis=1), jnp.concatenate([b, b_rest, b], axis=0),
        preferred_element_type=jnp.float32)


def project_kernel(top_ref, weighted_ref, modes_ref, projector, z_ref, load_sem):
    @pl.when(pl.program_id(0) == 0)
    def _():
        load = pltpu.make_async_copy(weighted_ref, z_ref, load_sem)
        load.start()
        width = top_ref.shape[1]
        half = width // 2
        out_cols = projector.shape[0]
        rows = lax.broadcasted_iota(jnp.int32, (width, width), 0)
        columns = lax.broadcasted_iota(jnp.int32, (width, width), 1)
        lift = jnp.where(rows == columns, 1.5, 0.0)
        iterates = []
        for f in range(FREQ):
            top = top_ref[f * half : (f + 1) * half]
            bottom = pltpu.roll(top, half, 1)
            bottom = jnp.where(columns[:half] < half, -bottom, bottom)
            full = jnp.concatenate([top, bottom], axis=0)
            norm = jnp.sqrt(jnp.sum(full * full, axis=(0, 1), keepdims=True) + 1e-06)
            iterates.append(full / norm)
        whiteners = [None] * FREQ
        for at in range(ITERS):
            for f in range(FREQ):
                both = iterates[f] if at == 0 else exact(whiteners[f], iterates[f])
                fix = lift - 0.5 * both
                if at < ITERS - 1:
                    iterates[f] = exact(iterates[f], fix)
                whiteners[f] = fix if at == 0 else exact(fix, whiteners[f])
        for f in range(FREQ):
            straight = jnp.where(rows < half, whiteners[f], -whiteners[f])
            crossed = pltpu.roll(whiteners[f], half, 0)
            shape = (width, out_cols)
            value = jnp.dot(
                straight.astype(jnp.bfloat16), spot(shape, 2 * f * RANK, 0, RANK),
                preferred_element_type=jnp.float32)
            value += jnp.dot(
                crossed.astype(jnp.bfloat16), spot(shape, (2 * f + 1) * RANK, 0, RANK),
                preferred_element_type=jnp.float32)
            projector[:, f * width : (f + 1) * width] = value.T.astype(jnp.bfloat16)
        load.wait()

    tile = modes_ref.shape[1]
    at = pl.multiple_of(pl.program_id(0) * tile, tile)

    modes_ref[...] = lax.dot_general(
        projector[...], z_ref[pl.ds(at, tile)], (((1,), (1,)), ((), ())),
        preferred_element_type=jnp.float32).astype(modes_ref.dtype)


def project_call(top, weighted):
    rows, cols = weighted.shape
    out_cols = FREQ * 2 * RANK
    tile = rows // 4
    return pl.pallas_call(
        project_kernel,
        grid=(rows // tile,),
        out_shape=jax.ShapeDtypeStruct((out_cols, rows), jnp.bfloat16),
        in_specs=[
            pl.BlockSpec(top.shape, lambda i: (0, 0)),
            pl.BlockSpec(memory_space=pl.ANY),
        ],
        out_specs=pl.BlockSpec((out_cols, tile), lambda i: (0, i)),
        scratch_shapes=[
            pltpu.VMEM((out_cols, cols), jnp.bfloat16),
            pltpu.VMEM((rows, cols), jnp.bfloat16),
            pltpu.SemaphoreType.DMA,
        ],
        compiler_params=pltpu.CompilerParams(
            vmem_limit_bytes=60 << 20, dimension_semantics=("arbitrary",)),
        name="project",
    )(top, weighted)


def local(n_row, n_sub, spectra, mass_blocks, offsets, counts):
    rows, cols = spectra.shape[1:]
    size = mass_blocks.shape[3]
    weighted, total = weigh_call(
        n_row, n_sub, counts, offsets.transpose(2, 0, 1),
        spectra[0].reshape(rows // size, size, cols), mass_blocks[0])
    width = cols // FREQ
    modes = project_call(
        total.reshape(FREQ * width // 2, width), weighted.reshape(rows, cols))
    return modes.T[None]


def solution(mesh):
    return jax.shard_map(
        functools.partial(local, mesh.shape["row"], mesh.shape["sub"]),
        mesh=mesh,
        in_specs=(
            P("sub", "row", None),
            P("sub", "row", None, None, None),
            P("sub", "row", None),
            P("sub"),
        ),
        out_specs=P("sub", "row", None),
        check_vma=False,
    )
```
